512 devices in a mesh: dp: 4 (over x), fsdp: 128 (over z, y, core).
Axes of the slice: x: 4, y: 8, z: 8, core: 2. Of those that a mesh axis runs over, the one named last changes fastest.
Arguments:
- grad_parts: bfloat16 [4, 384, 256, 256], P('dp', None, 'fsdp'), may hold values from -4 to 4
- owner_slot: int32 [4, 96], replicated, may hold values from 0 to 255, as said below
- moment: bfloat16 [1024, 256, 256], P(('dp', 'fsdp')), may hold values from -6 to 6
- second: float32 [1024, 256, 256], P(('dp', 'fsdp')), may hold values from 0.2 to 5
- gram_left: float32 [1024, 256, 256], P(('dp', 'fsdp')), may hold values from -24 to 24
- gram_right: float32 [1024, 256, 256], P(('dp', 'fsdp')), may hold values from -24 to 24
- basis_left: bfloat16 [1024, 256, 256], P(('dp', 'fsdp')), may hold values from -0.375 to 0.375
- basis_right: bfloat16 [1024, 256, 256], P(('dp', 'fsdp')), may hold values from -0.375 to 0.375
Outputs:
- new_moment: bfloat16 [1024, 256, 256], P(('dp', 'fsdp'))
- new_second: float32 [1024, 256, 256], P(('dp', 'fsdp'))
- new_left: float32 [1024, 256, 256], P(('dp', 'fsdp'))
- new_right: float32 [1024, 256, 256], P(('dp', 'fsdp'))
- update: bfloat16 [384, 256, 256], P(None, 'fsdp')
The draws below stay inside these ranges and needn't reach their ends.
Inputs may be any that keep to these rules, and one draw needn't show every extreme that they name: `owner_slot`: in each row the 96 entries are distinct; entry o * 2 + c names slot c of owner o along fsdp; in every row some owner receives 2 blocks.
All inputs are finite; a program needn't handle non-finite values.
Results may differ from the reference program's by a relative error of at most 0.01.
Values may be sent and summed in bfloat16 or wider, within the bound.
A program may use at most 64 MiB of HBM per device.

```python
import math
import jax
import jax.numpy as jnp
from jax import lax

SIDE = 256
CAPACITY = 2
GROUP_BLOCKS = 96
BLOCKS = 384
SLOTS = 1024
N_DP = 4
N_FSDP = 128


def owner_row(key):
    first_key, second_key = jax.random.split(key)
    slot_total = N_FSDP * CAPACITY
    shuffled = jax.random.permutation(first_key, slot_total).astype(jnp.int32)
    leader_owner = shuffled[0] // CAPACITY
    order_keys = (shuffled // CAPACITY != leader_owner).astype(jnp.int32)
    ordering = jnp.argsort(order_keys, stable=True)
    chosen = shuffled[ordering][:GROUP_BLOCKS]
    mixing = jax.random.permutation(second_key, GROUP_BLOCKS)
    return chosen[mixing].astype(jnp.int32)


def draw_owner_slot(key, part):
    key = jax.random.fold_in(key, 11)
    row_keys = jax.random.split(key, N_DP)
    return jax.vmap(owner_row)(row_keys).astype(jnp.int32)


def levels(rng, dims, pieces, smallest, largest):
    def one(dim, parts):
        steps = jax.random.uniform(jax.random.fold_in(jax.random.fold_in(rng, 6), dim), (parts,), jnp.float32, smallest / len(pieces), largest / len(pieces))
        return jnp.repeat(jnp.exp(steps), dims[dim] // parts).reshape((-1,) + (1,) * (len(dims) - dim - 1))

    gain = one(*pieces[0])
    for cut in pieces[1:]:
        gain = gain * one(*cut)
    return gain


def bell_draw(stream_key, extent, spread, limit, cuts=(), kind=jnp.bfloat16):
    array = spread * jax.random.normal(stream_key, extent, jnp.float32)
    if cuts:
        array = array * levels(stream_key, extent, cuts, -0.22, 0.18)
    return jnp.clip(array, -limit, limit).astype(kind)


def setup_inputs(seed: int = 0) -> dict:
    key_of = jax.random.split(jax.random.key(seed), 9)
    return {
        "grad_parts": bell_draw(key_of[0], (N_DP, BLOCKS, SIDE, SIDE), 0.5, 4.0, ((0, 4), (2, 128))),
        "owner_slot": draw_owner_slot(jax.random.fold_in(key_of[8], 71), 0),
        "moment": bell_draw(key_of[2], (SLOTS, SIDE, SIDE), 1.0, 6.0, ((0, 512),)),
        "second": jnp.clip(jnp.exp(math.log(5.0) - 3.218876 * jax.random.uniform(key_of[3], (SLOTS, SIDE, SIDE), jnp.float32) ** levels(key_of[3], (SLOTS, SIDE, SIDE), ((0, 512),), -0.2, 0.2)), 0.2, 5.0),
        "gram_left": bell_draw(key_of[4], (SLOTS, SIDE, SIDE), 4.0, 24.0, ((0, 512),), jnp.float32),
        "gram_right": bell_draw(key_of[5], (SLOTS, SIDE, SIDE), 4.0, 24.0, ((0, 512),), jnp.float32),
        "basis_left": bell_draw(key_of[6], (SLOTS, SIDE, SIDE), SIDE ** -0.5, 0.375, ((0, 512),)),
        "basis_right": bell_draw(key_of[7], (SLOTS, SIDE, SIDE), SIDE ** -0.5, 0.375, ((0, 512),)),
    }


def per_slot(operands):
    slot_grad, moment, second, gram_left, gram_right, basis_left, basis_right = operands
    rounded = slot_grad.astype(jnp.bfloat16)
    halfway = jnp.dot(basis_left.T, rounded, preferred_element_type=jnp.float32).astype(jnp.bfloat16)
    rotated = jnp.dot(halfway, basis_right, preferred_element_type=jnp.float32)
    new_left = 0.95 * gram_left + 0.05 * jnp.dot(slot_grad, slot_grad.T, precision=lax.Precision.HIGHEST)
    new_right = 0.95 * gram_right + 0.05 * jnp.dot(slot_grad.T, slot_grad, precision=lax.Precision.HIGHEST)
    first_moment = 0.95 * moment.astype(jnp.float32) + 0.05 * rotated
    new_second = 0.95 * second + 0.05 * rotated * rotated
    direct = (first_moment / (jnp.sqrt(new_second) + 1e-08)).astype(jnp.bfloat16)
    returned = jnp.dot(basis_left, direct, preferred_element_type=jnp.float32).astype(jnp.bfloat16)
    slot_update = jnp.dot(returned, basis_right.T, preferred_element_type=jnp.float32).astype(jnp.bfloat16)
    return (first_moment.astype(jnp.bfloat16), new_second, new_left, new_right, slot_update)

def reference(grad_parts, owner_slot, moment, second, gram_left, gram_right, basis_left, basis_right):
    summed = lax.optimization_barrier(jnp.sum(grad_parts.astype(jnp.float32), axis=0))
    slot_span = N_FSDP * CAPACITY
    slot_index = (owner_slot + jnp.arange(N_DP, dtype=jnp.int32)[:, None] * slot_span).reshape(-1).astype(jnp.int32)
    slot_grad = jnp.zeros((N_DP * slot_span, SIDE, SIDE), jnp.float32).at[slot_index].set(summed)
    new_moment, new_second, new_left, new_right, slot_update = lax.map(per_slot, (slot_grad, moment, second, gram_left, gram_right, basis_left, basis_right))
    update = slot_update[slot_index]
    return (new_moment, new_second, new_left, new_right, update)
```

```python
import functools

import jax
import jax.numpy as jnp
from jax import lax
from jax.experimental import pallas as pl
from jax.experimental.pallas import tpu as pltpu
from jax.sharding import PartitionSpec as P

MESH = pl.DeviceIdType.MESH
UNROLL = 8
TILE = 8


def contract(a, b, a_dim, b_dim):
    return lax.dot_general(
        a, b, (((a_dim,), (b_dim,)), ((), ())), preferred_element_type=jnp.float32
    )


def soap_kernel(
    dp_count,
    fsdp_count,
    block_of,
    owner_slot,
    grad_parts,
    moment,
    second,
    gram_left,
    gram_right,
    basis_left,
    basis_right,
    new_moment,
    new_second,
    new_left,
    new_right,
    update,
    moment_v,
    second_v,
    left_v,
    right_v,
    basis_left_v,
    basis_right_v,
    partials,
    summed,
    outgoing,
    incoming,
    slot_grad,
    slot_update,
    returning,
    returned,
    picked,
    load_sems,
    store_sems,
    partial_send,
    partial_recv,
    out_send,
    in_recv,
    back_send,
    back_recv,
    gather_send,
    gather_recv,
):
    dp = lax.axis_index("dp")
    me = lax.axis_index("fsdp")
    capacity, side = moment.shape[0], moment.shape[1]
    group_blocks = owner_slot.shape[1]
    rows = grad_parts.shape[2]

    own_partial = pltpu.make_async_copy(
        grad_parts.at[0, pl.ds(dp * group_blocks, group_blocks)], partials.at[0], load_sems.at[6]
    )
    own_partial.start()
    loads = [
        pltpu.make_async_copy(src, dst, load_sems.at[i])
        for i, (src, dst) in enumerate(
            (
                (basis_left, basis_left_v),
                (basis_right, basis_right_v),
                (moment, moment_v),
                (second, second_v),
                (gram_left, left_v),
                (gram_right, right_v),
            )
        )
    ]
    for load in loads:
        load.start()

    barrier = pltpu.get_barrier_semaphore()
    for k in range(1, dp_count):
        pl.semaphore_signal(
            barrier, inc=1, device_id=(lax.rem(dp + k, dp_count), me), device_id_type=MESH
        )

    def greet(k, carry):
        pl.semaphore_signal(
            barrier, inc=1, device_id=(dp, lax.rem(me + k, fsdp_count)), device_id_type=MESH
        )
        return carry

    lax.fori_loop(1, fsdp_count, greet, 0)
    pl.semaphore_wait(barrier, dp_count - 1 + fsdp_count - 1)

    partial_copies = []
    for k in range(1, dp_count):
        target = lax.rem(dp + k, dp_count)
        copy = pltpu.make_async_remote_copy(
            src_ref=grad_parts.at[0, pl.ds(target * group_blocks, group_blocks)],
            dst_ref=partials.at[k],
            send_sem=partial_send.at[k - 1],
            recv_sem=partial_recv.at[k - 1],
            device_id=(target, me),
            device_id_type=MESH,
        )
        copy.start()
        partial_copies.append(copy)
    summed[group_blocks] = jnp.zeros(summed.shape[1:], summed.dtype)
    own_partial.wait()
    for copy in partial_copies:
        copy.wait_recv()

    def add_up(i, carry):
        here = pl.ds(i * UNROLL, UNROLL)
        total = partials[0, here].astype(jnp.float32)
        for k in range(1, dp_count):
            total = total + partials[k, here].astype(jnp.float32)
        summed[here] = total.astype(jnp.bfloat16)
        return carry

    lax.fori_loop(0, group_blocks // UNROLL, add_up, 0)

    def send_out(k, carry):
        owner = lax.rem(me + k, fsdp_count)
        for c in range(capacity):
            slot = owner * capacity + c
            outgoing[slot] = summed[block_of[dp, slot]]
        here = pl.ds(owner * capacity, capacity)
        pltpu.make_async_remote_copy(
            src_ref=outgoing.at[here],
            dst_ref=incoming.at[pl.ds(me * capacity, capacity)],
            send_sem=out_send,
            recv_sem=in_recv,
            device_id=(dp, owner),
            device_id_type=MESH,
        ).start()
        return carry

    lax.fori_loop(1, fsdp_count, send_out, 0)
    for c in range(capacity):
        slot = me * capacity + c
        incoming[slot] = summed[block_of[dp, slot]]

    others = pl.ds(0, (fsdp_count - 1) * capacity)
    out_all = pltpu.make_async_remote_copy(
        src_ref=outgoing.at[others],
        dst_ref=incoming.at[others],
        send_sem=out_send,
        recv_sem=in_recv,
        device_id=(dp, lax.rem(me + 1, fsdp_count)),
        device_id_type=MESH,
    )
    out_all.wait_recv()

    per_tile = slot_grad.shape[2] // rows

    def unpack(i, carry):
        for u in range(per_tile):
            for c in range(capacity):
                slot_grad[c, i, u * rows : (u + 1) * rows, :] = incoming[
                    (i * per_tile + u) * capacity + c
                ].astype(jnp.float32)
        return carry

    lax.fori_loop(0, slot_grad.shape[1], unpack, 0)

    for load in loads:
        load.wait()

    rounded = [
        slot_grad[c].reshape(side, side).astype(jnp.bfloat16) for c in range(capacity)
    ]
    for c in range(capacity):
        halfway = contract(basis_left_v[c], rounded[c], 0, 0).astype(jnp.bfloat16)
        rotated = contract(halfway, basis_right_v[c], 1, 0)
        first_moment = 0.95 * moment_v[c].astype(jnp.float32) + 0.05 * rotated
        moment_v[c] = first_moment.astype(jnp.bfloat16)
        second_moment = 0.95 * second_v[c] + 0.05 * rotated * rotated
        second_v[c] = second_moment
        direct = (first_moment / (jnp.sqrt(second_moment) + 1e-8)).astype(jnp.bfloat16)
        back = contract(basis_left_v[c], direct, 1, 0).astype(jnp.bfloat16)
        slot_update[c] = contract(back, basis_right_v[c], 1, 1).reshape(slot_update.shape[1:])

    def pack(i, carry):
        for u in range(per_tile):
            for c in range(capacity):
                returning[(i * per_tile + u) * capacity + c] = slot_update[
                    c, i, u * rows : (u + 1) * rows, :
                ].astype(jnp.bfloat16)
        return carry

    lax.fori_loop(0, slot_update.shape[1], pack, 0)

    def send_back(k, carry):
        target = lax.rem(me + k, fsdp_count)
        here = pl.ds(target * capacity, capacity)
        pltpu.make_async_remote_copy(
            src_ref=returning.at[here],
            dst_ref=returned.at[pl.ds(me * capacity, capacity)],
            send_sem=back_send,
            recv_sem=back_recv,
            device_id=(dp, target),
            device_id_type=MESH,
        ).start()
        return carry

    lax.fori_loop(1, fsdp_count, send_back, 0)
    for c in range(capacity):
        returned[me * capacity + c] = returning[me * capacity + c]

    stores = [
        pltpu.make_async_copy(moment_v, new_moment, store_sems.at[0]),
        pltpu.make_async_copy(second_v, new_second, store_sems.at[1]),
        pltpu.make_async_copy(left_v, new_left, store_sems.at[2]),
        pltpu.make_async_copy(right_v, new_right, store_sems.at[3]),
    ]
    stores[0].start()
    stores[1].start()
    for c in range(capacity):
        left_v[c] = 0.95 * left_v[c] + 0.05 * contract(rounded[c], rounded[c], 1, 1)
        right_v[c] = 0.95 * right_v[c] + 0.05 * contract(rounded[c], rounded[c], 0, 0)
    stores[2].start()
    stores[3].start()

    back_all = pltpu.make_async_remote_copy(
        src_ref=returning.at[others],
        dst_ref=returned.at[others],
        send_sem=back_send,
        recv_sem=back_recv,
        device_id=(dp, lax.rem(me + 1, fsdp_count)),
        device_id_type=MESH,
    )
    back_all.wait_recv()

    def pick(i, carry):
        for u in range(UNROLL):
            j = i * UNROLL + u
            picked[j] = returned[owner_slot[dp, j]]
        return carry

    lax.fori_loop(0, group_blocks // UNROLL, pick, 0)

    mine = pl.ds(dp * group_blocks, group_blocks)
    gathers = []
    for k in range(1, dp_count):
        copy = pltpu.make_async_remote_copy(
            src_ref=picked,
            dst_ref=update.at[mine],
            send_sem=gather_send.at[k - 1],
            recv_sem=gather_recv.at[k - 1],
            device_id=(lax.rem(dp + k, dp_count), me),
            device_id_type=MESH,
        )
        copy.start()
        gathers.append(copy)
    keep = pltpu.make_async_copy(picked, update.at[mine], store_sems.at[4])
    keep.start()
    out_all.wait_send()
    back_all.wait_send()
    for copy in partial_copies:
        copy.wait_send()
    for store in stores:
        store.wait()
    keep.wait()
    for copy in gathers:
        copy.wait()


def on_device(
    dp_count,
    fsdp_count,
    grad_parts,
    owner_slot,
    moment,
    second,
    gram_left,
    gram_right,
    basis_left,
    basis_right,
):
    capacity, side = moment.shape[0], moment.shape[1]
    blocks, rows = grad_parts.shape[1], grad_parts.shape[2]
    group_blocks = owner_slot.shape[1]
    slots = fsdp_count * capacity
    filled = owner_slot[:, None, :] == jnp.arange(slots, dtype=jnp.int32)[None, :, None]
    block_of = jnp.min(
        jnp.where(filled, jnp.arange(group_blocks, dtype=jnp.int32)[None, None, :], group_blocks),
        axis=2,
    )
    any_spec = pl.BlockSpec(memory_space=pl.ANY)
    smem_spec = pl.BlockSpec(memory_space=pltpu.SMEM)
    square = (capacity, side, side)
    tiled = (capacity, side // TILE, TILE, side)
    dma = pltpu.SemaphoreType.DMA
    return pl.pallas_call(
        functools.partial(soap_kernel, dp_count, fsdp_count),
        out_shape=(
            jax.ShapeDtypeStruct(square, jnp.bfloat16),
            jax.ShapeDtypeStruct(square, jnp.float32),
            jax.ShapeDtypeStruct(square, jnp.float32),
            jax.ShapeDtypeStruct(square, jnp.float32),
            jax.ShapeDtypeStruct((blocks, rows, side), jnp.bfloat16),
        ),
        in_specs=[smem_spec, smem_spec] + [any_spec] * 7,
        out_specs=[any_spec] * 5,
        scratch_shapes=[
            pltpu.VMEM(square, jnp.bfloat16),
            pltpu.VMEM(square, jnp.float32),
            pltpu.VMEM(square, jnp.float32),
            pltpu.VMEM(square, jnp.float32),
            pltpu.VMEM(square, jnp.bfloat16),
            pltpu.VMEM(square, jnp.bfloat16),
            pltpu.VMEM((dp_count, group_blocks, rows, side), jnp.bfloat16),
            pltpu.VMEM((group_blocks + 1, rows, side), jnp.bfloat16),
            pltpu.VMEM((slots, rows, side), jnp.bfloat16),
            pltpu.VMEM((slots, rows, side), jnp.bfloat16),
            pltpu.VMEM(tiled, jnp.float32),
            pltpu.VMEM(tiled, jnp.float32),
            pltpu.VMEM((slots, rows, side), jnp.bfloat16),
            pltpu.VMEM((slots, rows, side), jnp.bfloat16),
            pltpu.VMEM((group_blocks, rows, side), jnp.bfloat16),
            dma((7,)),
            dma((5,)),
            dma((dp_count - 1,)),
            dma((dp_count - 1,)),
            dma,
            dma,
            dma,
            dma,
            dma((dp_count - 1,)),
            dma((dp_count - 1,)),
        ],
        compiler_params=pltpu.CompilerParams(
            collective_id=0, has_side_effects=True, vmem_limit_bytes=32 * 1024 * 1024
        ),
    )(
        block_of,
        owner_slot,
        grad_parts,
        moment,
        second,
        gram_left,
        gram_right,
        basis_left,
        basis_right,
    )


def solution(mesh):
    by_slot = P(("dp", "fsdp"), None, None)
    return jax.shard_map(
        functools.partial(on_device, mesh.shape["dp"], mesh.shape["fsdp"]),
        mesh=mesh,
        in_specs=(P("dp", None, "fsdp", None), P()) + (by_slot,) * 6,
        out_specs=(by_slot,) * 4 + (P(None, "fsdp", None),),
        check_vma=False,
    )
```

```python
import functools
import math

import jax
import jax.numpy as jnp
from jax import lax
from jax.experimental import pallas as pl
from jax.experimental.pallas import tpu as pltpu
from jax.sharding import PartitionSpec as P

MESH = pl.DeviceIdType.MESH
UNROLL = 8
TILE = 8
LANES = 128
LIMIT = 60


def contract(a, b, a_dim, b_dim):
    return lax.dot_general(
        a, b, (((a_dim,), (b_dim,)), ((), ())), preferred_element_type=jnp.float32
    )


class Exchange:
    def __init__(self, dp, me, far, near, bufs, sems):
        self.dp, self.far, self.near = dp, far, near
        self.z, self.a = lax.div(me, near), lax.rem(me, near)
        self.out0, self.mid0, self.in0, self.out1, self.mid1, self.in1 = bufs
        self.sems = sems

    def copy(self, src, dst, which, z, a):
        return pltpu.make_async_remote_copy(
            src_ref=src,
            dst_ref=dst,
            send_sem=self.sems.at[2 * which],
            recv_sem=self.sems.at[2 * which + 1],
            device_id=(self.dp, z * self.near + a),
            device_id_type=MESH,
        )

    def whole(self, which):
        buf = (self.mid0, self.mid1, self.in0, self.in1)[which]
        others = buf.at[pl.ds(0, buf.shape[0] - 1)]
        return self.copy(others, others, which, self.z, lax.rem(self.a + 1, self.near))

    def own(self, src, dst, which):
        return pltpu.make_async_copy(src, dst, self.sems.at[8 + which])

    def first_hop(self, piece):
        def fill0(z, carry):
            for a in range(self.near):
                self.out0[a, z] = piece(0, z, a)
            return carry

        lax.fori_loop(0, self.far, fill0, 0)

        def send0(k, carry):
            a = lax.rem(self.a + k, self.near)
            self.copy(self.out0.at[a], self.mid0.at[self.a], 0, self.z, a).start()
            return carry

        lax.fori_loop(1, self.near, send0, 0)
        self.own(self.out0.at[self.a], self.mid0.at[self.a], 0).start()

        def fill1(z):
            for a in range(self.near):
                self.out1[z, a] = piece(1, z, a)

        def send1(k, carry):
            z = lax.rem(self.z + k, self.far)
            fill1(z)
            self.copy(self.out1.at[z], self.mid1.at[self.z], 1, z, self.a).start()
            return carry

        lax.fori_loop(1, self.far, send1, 0)
        fill1(self.z)
        self.own(self.out1.at[self.z], self.mid1.at[self.z], 1).start()

    def second_hop(self):
        self.own(self.out0.at[self.a], self.mid0.at[self.a], 0).wait()
        self.whole(0).wait_recv()

        def send0(k, carry):
            z = lax.rem(self.z + k, self.far)
            self.copy(self.mid0.at[:, z], self.in0.at[self.z], 2, z, self.a).start()
            return carry

        lax.fori_loop(1, self.far, send0, 0)
        self.own(self.mid0.at[:, self.z], self.in0.at[self.z], 2).start()

        self.own(self.out1.at[self.z], self.mid1.at[self.z], 1).wait()
        self.whole(1).wait_recv()

        def send1(k, carry):
            a = lax.rem(self.a + k, self.near)
            self.copy(self.mid1.at[:, a], self.in1.at[self.a], 3, self.z, a).start()
            return carry

        lax.fori_loop(1, self.near, send1, 0)
        self.own(self.mid1.at[:, self.a], self.in1.at[self.a], 3).start()

    def wait_slot(self, slot):
        if slot == 0:
            self.own(self.mid0.at[:, self.z], self.in0.at[self.z], 2).wait()
        else:
            self.own(self.mid1.at[:, self.a], self.in1.at[self.a], 3).wait()
        self.whole(2 + slot).wait_recv()

    def arrived(self, slot, z, a):
        return self.in0[z, a] if slot == 0 else self.in1[a, z]

    def finish(self):
        for which in range(4):
            self.whole(which).wait_send()


def soap_kernel(
    dp_count,
    far,
    near,
    owner_slot,
    grad_parts,
    moment,
    second,
    gram_left,
    gram_right,
    basis_left,
    basis_right,
    new_moment,
    new_second,
    new_left,
    new_right,
    update,
    owner_s,
    block_v,
    block_s,
    moment_v,
    second_v,
    left_v,
    right_v,
    basis_left_v,
    basis_right_v,
    partials,
    summed,
    slot_grad,
    slot_update,
    picked,
    load_sems,
    keep_sem,
    partial_send,
    partial_recv,
    gather_send,
    gather_recv,
    out_sems,
    back_sems,
    *buffers,
):
    dp = lax.axis_index("dp")
    me = lax.axis_index("fsdp")
    capacity, side = moment.shape[0], moment.shape[1]
    group_blocks = owner_slot.shape[1]
    rows = grad_parts.shape[2]
    my_z, my_a = lax.div(me, near), lax.rem(me, near)
    outward = Exchange(dp, me, far, near, buffers[:6], out_sems)
    backward = Exchange(dp, me, far, near, buffers[6:], back_sems)

    barrier = pltpu.get_barrier_semaphore()

    def greet(d, f):
        pl.semaphore_signal(barrier, inc=1, device_id=(d, f), device_id_type=MESH)

    for k in range(1, dp_count):
        greet(lax.rem(dp + k, dp_count), me)
    for k in range(1, near):
        greet(dp, my_z * near + lax.rem(my_a + k, near))
    for k in range(1, far):
        greet(dp, lax.rem(my_z + k, far) * near + my_a)

    own_partial = pltpu.make_async_copy(
        grad_parts.at[0, pl.ds(dp * group_blocks, group_blocks)], partials.at[0], load_sems.at[6]
    )
    own_partial.start()
    own_owners = pltpu.make_async_copy(owner_slot, owner_s, load_sems.at[7])
    own_owners.start()
    loads = [
        pltpu.make_async_copy(src, dst, load_sems.at[i])
        for i, (src, dst) in enumerate(
            (
                (basis_left, basis_left_v),
                (basis_right, basis_right_v),
                (moment, moment_v),
                (second, second_v),
                (gram_left, left_v),
                (gram_right, right_v),
            )
        )
    ]
    for load in loads:
        load.start()
    pl.semaphore_wait(barrier, dp_count - 1 + near - 1 + far - 1)

    partial_copies = []
    for k in range(1, dp_count):
        target = lax.rem(dp + k, dp_count)
        copy = pltpu.make_async_remote_copy(
            src_ref=grad_parts.at[0, pl.ds(target * group_blocks, group_blocks)],
            dst_ref=partials.at[k],
            send_sem=partial_send.at[k - 1],
            recv_sem=partial_recv.at[k - 1],
            device_id=(target, me),
            device_id_type=MESH,
        )
        copy.start()
        partial_copies.append(copy)

    own_owners.wait()
    summed[group_blocks] = jnp.zeros(summed.shape[1:], summed.dtype)
    row_slots = near * capacity
    lane = lax.broadcasted_iota(jnp.int32, block_v.shape, 1)
    slot_id = row_slots * lax.broadcasted_iota(jnp.int32, block_v.shape, 0) + lane
    slot_id = jnp.where(lane < row_slots, slot_id, -1)

    def note(i, table):
        for u in range(UNROLL):
            j = i * UNROLL + u
            table = jnp.where(slot_id == owner_s[dp, j], j, table)
        return table

    block_v[...] = lax.fori_loop(
        0, group_blocks // UNROLL, note, jnp.full(block_v.shape, group_blocks, jnp.int32)
    )
    table_copy = pltpu.make_async_copy(block_v, block_s, load_sems.at[8])
    table_copy.start()

    own_partial.wait()
    for copy in partial_copies:
        copy.wait_recv()

    def add_up(i, carry):
        here = pl.ds(i * UNROLL, UNROLL)
        total = partials[0, here].astype(jnp.float32)
        for k in range(1, dp_count):
            total = total + partials[k, here].astype(jnp.float32)
        summed[here] = total.astype(jnp.bfloat16)
        return carry

    lax.fori_loop(0, group_blocks // UNROLL, add_up, 0)
    table_copy.wait()

    def grad_piece(c, z, a):
        return summed[block_s[z, a * capacity + c]]

    outward.first_hop(grad_piece)
    outward.second_hop()

    per_tile = TILE // rows
    tiles_near = near // per_tile

    def unpack(c):
        def far_rows(z, carry):
            for a in range(near):
                u = a % per_tile
                slot_grad[c, z * tiles_near + a // per_tile, u * rows : (u + 1) * rows, :] = (
                    outward.arrived(c, z, a).astype(jnp.float32)
                )
            return carry

        lax.fori_loop(0, far, far_rows, 0)

    for load in loads:
        load.wait()

    rounded = []
    for c in range(capacity):
        outward.wait_slot(c)
        unpack(c)
        rounded.append(slot_grad[c].reshape(side, side).astype(jnp.bfloat16))
        halfway = contract(basis_left_v[c], rounded[c], 0, 0).astype(jnp.bfloat16)
        rotated = contract(halfway, basis_right_v[c], 1, 0)
        first_moment = 0.95 * moment_v[c].astype(jnp.float32) + 0.05 * rotated
        new_moment[c] = first_moment.astype(jnp.bfloat16)
        second_moment = 0.95 * second_v[c] + 0.05 * rotated * rotated
        new_second[c] = second_moment
        direct = (first_moment / (jnp.sqrt(second_moment) + 1e-8)).astype(jnp.bfloat16)
        back = contract(basis_left_v[c], direct, 1, 0).astype(jnp.bfloat16)
        slot_update[c] = contract(back, basis_right_v[c], 1, 1).reshape(slot_update.shape[1:])

    def update_piece(c, z, a):
        u = a % per_tile
        return slot_update[
            c, z * tiles_near + a // per_tile, u * rows : (u + 1) * rows, :
        ].astype(jnp.bfloat16)

    backward.first_hop(update_piece)

    for c in range(capacity):
        new_left[c] = 0.95 * left_v[c] + 0.05 * contract(rounded[c], rounded[c], 1, 1)
        new_right[c] = 0.95 * right_v[c] + 0.05 * contract(rounded[c], rounded[c], 0, 0)
    backward.second_hop()
    for c in range(capacity):
        backward.wait_slot(c)

    def pick(i, carry):
        for u in range(UNROLL):
            j = i * UNROLL + u
            slot = owner_s[dp, j]
            owner = lax.div(slot, capacity)
            z, a = lax.div(owner, near), lax.rem(owner, near)
            first, other = backward.arrived(0, z, a), backward.arrived(1, z, a)
            picked[j] = jnp.where(lax.rem(slot, capacity) == 0, first, other)
        return carry

    lax.fori_loop(0, group_blocks // UNROLL, pick, 0)

    mine = pl.ds(dp * group_blocks, group_blocks)
    gathers = []
    for k in range(1, dp_count):
        copy = pltpu.make_async_remote_copy(
            src_ref=picked,
            dst_ref=update.at[mine],
            send_sem=gather_send.at[k - 1],
            recv_sem=gather_recv.at[k - 1],
            device_id=(lax.rem(dp + k, dp_count), me),
            device_id_type=MESH,
        )
        copy.start()
        gathers.append(copy)
    keep = pltpu.make_async_copy(picked, update.at[mine], keep_sem)
    keep.start()
    outward.finish()
    backward.finish()
    for copy in partial_copies:
        copy.wait_send()
    keep.wait()
    for copy in gathers:
        copy.wait()


def hand_out_kernel(*refs):
    count = len(refs) // 2
    sems = refs[-1]
    copies = [
        pltpu.make_async_copy(src, dst, sems.at[i])
        for i, (src, dst) in enumerate(zip(refs[:count], refs[count : 2 * count]))
    ]
    for copy in copies:
        copy.start()
    for copy in copies:
        copy.wait()


def on_device(
    dp_count,
    fsdp_count,
    grad_parts,
    owner_slot,
    moment,
    second,
    gram_left,
    gram_right,
    basis_left,
    basis_right,
):
    capacity, side = moment.shape[0], moment.shape[1]
    blocks, rows = grad_parts.shape[1], grad_parts.shape[2]
    group_blocks = owner_slot.shape[1]
    far = math.isqrt(fsdp_count // 2)
    near = fsdp_count // far
    any_spec = pl.BlockSpec(memory_space=pl.ANY)
    square = (capacity, side, side)
    tiled = (capacity, side // TILE, TILE, side)
    near_far = pltpu.VMEM((near, far, rows, side), jnp.bfloat16)
    far_near = pltpu.VMEM((far, near, rows, side), jnp.bfloat16)
    table = (-(-far // TILE) * TILE, LANES)
    dma = pltpu.SemaphoreType.DMA
    out_shape = (
        jax.ShapeDtypeStruct(square, jnp.bfloat16),
        jax.ShapeDtypeStruct(square, jnp.float32),
        jax.ShapeDtypeStruct(square, jnp.float32),
        jax.ShapeDtypeStruct(square, jnp.float32),
        jax.ShapeDtypeStruct((blocks, rows, side), jnp.bfloat16),
    )
    results = pl.pallas_call(
        functools.partial(soap_kernel, dp_count, far, near),
        out_shape=tuple(pltpu.VMEM(out.shape, out.dtype) for out in out_shape),
        in_specs=[any_spec] * 8,
        out_specs=[pl.BlockSpec(memory_space=pltpu.VMEM)] * 5,
        scratch_shapes=[
            pltpu.SMEM(owner_slot.shape, jnp.int32),
            pltpu.VMEM(table, jnp.int32),
            pltpu.SMEM(table, jnp.int32),
            pltpu.VMEM(square, jnp.bfloat16),
            pltpu.VMEM(square, jnp.float32),
            pltpu.VMEM(square, jnp.float32),
            pltpu.VMEM(square, jnp.float32),
            pltpu.VMEM(square, jnp.bfloat16),
            pltpu.VMEM(square, jnp.bfloat16),
            pltpu.VMEM((dp_count, group_blocks, rows, side), jnp.bfloat16),
            pltpu.VMEM((group_blocks + 1, rows, side), jnp.bfloat16),
            pltpu.VMEM(tiled, jnp.float32),
            pltpu.VMEM(tiled, jnp.float32),
            pltpu.VMEM((group_blocks, rows, side), jnp.bfloat16),
            dma((9,)),
            dma,
            dma((dp_count - 1,)),
            dma((dp_count - 1,)),
            dma((dp_count - 1,)),
            dma((dp_count - 1,)),
            dma((12,)),
            dma((12,)),
        ]
        + [near_far, near_far, far_near, far_near, far_near, near_far] * 2,
        compiler_params=pltpu.CompilerParams(
            collective_id=0, has_side_effects=True, vmem_limit_bytes=LIMIT * 1024 * 1024
        ),
    )(
        owner_slot,
        grad_parts,
        moment,
        second,
        gram_left,
        gram_right,
        basis_left,
        basis_right,
    )
    return pl.pallas_call(
        hand_out_kernel,
        out_shape=out_shape,
        in_specs=[any_spec] * 5,
        out_specs=[any_spec] * 5,
        scratch_shapes=[dma((5,))],
        compiler_params=pltpu.CompilerParams(vmem_limit_bytes=8 * 1024 * 1024),
    )(*results)


def solution(mesh):
    by_slot = P(("dp", "fsdp"), None, None)
    return jax.shard_map(
        functools.partial(on_device, mesh.shape["dp"], mesh.shape["fsdp"]),
        mesh=mesh,
        in_specs=(P("dp", None, "fsdp", None), P()) + (by_slot,) * 6,
        out_specs=(by_slot,) * 4 + (P(None, "fsdp", None),),
        check_vma=False,
    )
```

```python
import functools
import math

import jax
import jax.numpy as jnp
from jax import lax
from jax.experimental import pallas as pl
from jax.experimental.pallas import tpu as pltpu
from jax.sharding import PartitionSpec as P

MESH = pl.DeviceIdType.MESH
UNROLL = 8
TILE = 8
LANES = 128
LIMIT = 60


def contract(a, b, a_dim, b_dim):
    return lax.dot_general(
        a, b, (((a_dim,), (b_dim,)), ((), ())), preferred_element_type=jnp.float32
    )


def farthest_first(count, i):
    out = lax.div(i + 1, 2)
    return lax.rem(count // 2 + out * (1 - 2 * lax.rem(i, 2)) + count, count)


class Exchange:
    def __init__(self, dp, me, far, near, outgoing, incoming, sems):
        self.dp, self.me, self.far, self.near = dp, me, far, near
        self.outgoing, self.incoming, self.sems = outgoing, incoming, sems
        self.span = outgoing.shape[0] // (far * near)

    def copy(self, src, dst, target):
        return pltpu.make_async_remote_copy(
            src_ref=src,
            dst_ref=dst,
            send_sem=self.sems.at[0],
            recv_sem=self.sems.at[1],
            device_id=(self.dp, target),
            device_id_type=MESH,
        )

    def send(self, z, a):
        target = z * self.near + a
        self.copy(
            self.outgoing.at[pl.ds(target * self.span, self.span)],
            self.incoming.at[pl.ds(self.me * self.span, self.span)],
            target,
        ).start()

    def start(self, fill):
        chips = self.near // 2
        my_z, my_a = lax.div(self.me, self.near), lax.rem(self.me, self.near)
        my_y, my_core = lax.div(my_a, 2), lax.rem(my_a, 2)
        for total in range(self.far + chips - 1):

            def step(i, carry):
                z = lax.rem(my_z + farthest_first(self.far, i), self.far)
                y = lax.rem(my_y + farthest_first(chips, total - i), chips)
                for core in (1 - my_core, my_core):
                    fill(z, 2 * y + core)
                    self.send(z, 2 * y + core)
                return carry

            low, high = max(0, total - chips + 1), min(self.far - 1, total)
            if total < self.far + chips - 2:
                lax.fori_loop(low, high + 1, step, 0)
        fill(my_z, 2 * my_y + 1 - my_core)
        self.send(my_z, 2 * my_y + 1 - my_core)
        fill(my_z, my_a)
        for c in range(self.span):
            self.incoming[self.me * self.span + c] = self.outgoing[self.me * self.span + c]

    def whole(self):
        others = self.incoming.at[pl.ds(0, (self.far * self.near - 1) * self.span)]
        return self.copy(others, others, lax.rem(self.me + 1, self.far * self.near))


def soap_kernel(
    dp_count,
    far,
    near,
    owner_slot,
    grad_parts,
    moment,
    second,
    gram_left,
    gram_right,
    basis_left,
    basis_right,
    new_moment,
    new_second,
    new_left,
    new_right,
    update,
    owner_s,
    block_v,
    block_s,
    moment_v,
    second_v,
    left_v,
    right_v,
    basis_left_v,
    basis_right_v,
    partials,
    summed,
    slot_grad,
    slot_update,
    picked,
    load_sems,
    keep_sem,
    partial_send,
    partial_recv,
    gather_send,
    gather_recv,
    ready,
    out_sems,
    back_sems,
    outgoing,
    incoming,
    returning,
    returned,
):
    dp = lax.axis_index("dp")
    me = lax.axis_index("fsdp")
    capacity, side = moment.shape[0], moment.shape[1]
    group_blocks = owner_slot.shape[1]
    rows = grad_parts.shape[2]
    my_z, my_a = lax.div(me, near), lax.rem(me, near)
    outward = Exchange(dp, me, far, near, outgoing, incoming, out_sems)
    backward = Exchange(dp, me, far, near, returning, returned, back_sems)

    barrier = pltpu.get_barrier_semaphore()

    def greet(d, f):
        pl.semaphore_signal(barrier, inc=1, device_id=(d, f), device_id_type=MESH)

    for k in range(1, dp_count):
        greet(lax.rem(dp + k, dp_count), me)
    for k in range(1, near):
        greet(dp, my_z * near + lax.rem(my_a + k, near))
    for k in range(1, far):
        greet(dp, lax.rem(my_z + k, far) * near + my_a)

    own_partial = pltpu.make_async_copy(
        grad_parts.at[0, pl.ds(dp * group_blocks, group_blocks)], partials.at[0], load_sems.at[6]
    )
    own_partial.start()
    own_owners = pltpu.make_async_copy(owner_slot, owner_s, load_sems.at[7])
    own_owners.start()
    loads = [
        pltpu.make_async_copy(src, dst, load_sems.at[i])
        for i, (src, dst) in enumerate(
            (
                (basis_left, basis_left_v),
                (basis_right, basis_right_v),
                (moment, moment_v),
                (second, second_v),
                (gram_left, left_v),
                (gram_right, right_v),
            )
        )
    ]
    for load in loads:
        load.start()
    pl.semaphore_wait(barrier, dp_count - 1 + near - 1 + far - 1)

    dp_offsets = sorted(range(1, dp_count), key=lambda k: -min(k, dp_count - k))
    partial_copies = []
    for k in dp_offsets:
        target = lax.rem(dp + k, dp_count)
        copy = pltpu.make_async_remote_copy(
            src_ref=grad_parts.at[0, pl.ds(target * group_blocks, group_blocks)],
            dst_ref=partials.at[k],
            send_sem=partial_send.at[k - 1],
            recv_sem=partial_recv.at[k - 1],
            device_id=(target, me),
            device_id_type=MESH,
        )
        copy.start()
        partial_copies.append(copy)

    for k in range(1, near):
        pl.semaphore_signal(
            ready,
            inc=1,
            device_id=(dp, my_z * near + lax.rem(my_a + k, near)),
            device_id_type=MESH,
        )

    own_owners.wait()
    summed[group_blocks] = jnp.zeros(summed.shape[1:], summed.dtype)
    row_slots = near * capacity
    lane = lax.broadcasted_iota(jnp.int32, block_v.shape, 1)
    slot_id = row_slots * lax.broadcasted_iota(jnp.int32, block_v.shape, 0) + lane
    slot_id = jnp.where(lane < row_slots, slot_id, -1)

    def note(i, table):
        for u in range(UNROLL):
            j = i * UNROLL + u
            table = jnp.where(slot_id == owner_s[dp, j], j, table)
        return table

    block_v[...] = lax.fori_loop(
        0, group_blocks // UNROLL, note, jnp.full(block_v.shape, group_blocks, jnp.int32)
    )
    table_copy = pltpu.make_async_copy(block_v, block_s, load_sems.at[8])
    table_copy.start()

    own_partial.wait()
    for copy in partial_copies:
        copy.wait_recv()

    def add_up(i, carry):
        here = pl.ds(i * UNROLL, UNROLL)
        total = partials[0, here].astype(jnp.float32)
        for k in range(1, dp_count):
            total = total + partials[k, here].astype(jnp.float32)
        summed[here] = total.astype(jnp.bfloat16)
        return carry

    lax.fori_loop(0, group_blocks // UNROLL, add_up, 0)
    table_copy.wait()

    pl.semaphore_wait(ready, near - 1)

    def fill_grad(z, a):
        for c in range(capacity):
            outgoing[(z * near + a) * capacity + c] = summed[block_s[z, a * capacity + c]]

    outward.start(fill_grad)

    per_tile = TILE // rows
    tiles_near = near // per_tile

    def unpack(z, carry):
        for a in range(near):
            u = a % per_tile
            for c in range(capacity):
                slot_grad[c, z * tiles_near + a // per_tile, u * rows : (u + 1) * rows, :] = incoming[
                    (z * near + a) * capacity + c
                ].astype(jnp.float32)
        return carry

    for load in loads:
        load.wait()
    outward.whole().wait_recv()
    lax.fori_loop(0, far, unpack, 0)

    rounded = []
    for c in range(capacity):
        rounded.append(slot_grad[c].reshape(side, side).astype(jnp.bfloat16))
        halfway = contract(basis_left_v[c], rounded[c], 0, 0).astype(jnp.bfloat16)
        rotated = contract(halfway, basis_right_v[c], 1, 0)
        first_moment = 0.95 * moment_v[c].astype(jnp.float32) + 0.05 * rotated
        new_moment[c] = first_moment.astype(jnp.bfloat16)
        second_moment = 0.95 * second_v[c] + 0.05 * rotated * rotated
        new_second[c] = second_moment
        direct = (first_moment / (jnp.sqrt(second_moment) + 1e-8)).astype(jnp.bfloat16)
        back = contract(basis_left_v[c], direct, 1, 0).astype(jnp.bfloat16)
        slot_update[c] = contract(back, basis_right_v[c], 1, 1).reshape(slot_update.shape[1:])

    def pack(z, carry):
        for a in range(near):
            u = a % per_tile
            for c in range(capacity):
                returning[(z * near + a) * capacity + c] = slot_update[
                    c, z * tiles_near + a // per_tile, u * rows : (u + 1) * rows, :
                ].astype(jnp.bfloat16)
        return carry

    lax.fori_loop(0, far, pack, 0)
    backward.start(lambda z, a: None)

    for c in range(capacity):
        new_left[c] = 0.95 * left_v[c] + 0.05 * contract(rounded[c], rounded[c], 1, 1)
        new_right[c] = 0.95 * right_v[c] + 0.05 * contract(rounded[c], rounded[c], 0, 0)
    backward.whole().wait_recv()

    def pick(i, carry):
        for u in range(UNROLL):
            picked[i * UNROLL + u] = returned[owner_s[dp, i * UNROLL + u]]
        return carry

    lax.fori_loop(0, group_blocks // UNROLL, pick, 0)

    mine = pl.ds(dp * group_blocks, group_blocks)
    gathers = []
    for k in dp_offsets:
        copy = pltpu.make_async_remote_copy(
            src_ref=picked,
            dst_ref=update.at[mine],
            send_sem=gather_send.at[k - 1],
            recv_sem=gather_recv.at[k - 1],
            device_id=(lax.rem(dp + k, dp_count), me),
            device_id_type=MESH,
        )
        copy.start()
        gathers.append(copy)
    keep = pltpu.make_async_copy(picked, update.at[mine], keep_sem)
    keep.start()
    outward.whole().wait_send()
    backward.whole().wait_send()
    for copy in partial_copies:
        copy.wait_send()
    keep.wait()
    for copy in gathers:
        copy.wait()


def hand_out_kernel(*refs):
    count = len(refs) // 2
    sems = refs[-1]
    copies = [
        pltpu.make_async_copy(src, dst, sems.at[i])
        for i, (src, dst) in enumerate(zip(refs[:count], refs[count : 2 * count]))
    ]
    for copy in copies:
        copy.start()
    for copy in copies:
        copy.wait()


def on_device(
    dp_count,
    fsdp_count,
    grad_parts,
    owner_slot,
    moment,
    second,
    gram_left,
    gram_right,
    basis_left,
    basis_right,
):
    capacity, side = moment.shape[0], moment.shape[1]
    blocks, rows = grad_parts.shape[1], grad_parts.shape[2]
    group_blocks = owner_slot.shape[1]
    far = math.isqrt(fsdp_count // 2)
    near = fsdp_count // far
    any_spec = pl.BlockSpec(memory_space=pl.ANY)
    square = (capacity, side, side)
    tiled = (capacity, side // TILE, TILE, side)
    by_slot = pltpu.VMEM((fsdp_count * capacity, rows, side), jnp.bfloat16)
    table = (-(-far // TILE) * TILE, LANES)
    dma = pltpu.SemaphoreType.DMA
    out_shape = (
        jax.ShapeDtypeStruct(square, jnp.bfloat16),
        jax.ShapeDtypeStruct(square, jnp.float32),
        jax.ShapeDtypeStruct(square, jnp.float32),
        jax.ShapeDtypeStruct(square, jnp.float32),
        jax.ShapeDtypeStruct((blocks, rows, side), jnp.bfloat16),
    )
    results = pl.pallas_call(
        functools.partial(soap_kernel, dp_count, far, near),
        out_shape=tuple(pltpu.VMEM(out.shape, out.dtype) for out in out_shape),
        in_specs=[any_spec] * 8,
        out_specs=[pl.BlockSpec(memory_space=pltpu.VMEM)] * 5,
        scratch_shapes=[
            pltpu.SMEM(owner_slot.shape, jnp.int32),
            pltpu.VMEM(table, jnp.int32),
            pltpu.SMEM(table, jnp.int32),
            pltpu.VMEM(square, jnp.bfloat16),
            pltpu.VMEM(square, jnp.float32),
            pltpu.VMEM(square, jnp.float32),
            pltpu.VMEM(square, jnp.float32),
            pltpu.VMEM(square, jnp.bfloat16),
            pltpu.VMEM(square, jnp.bfloat16),
            pltpu.VMEM((dp_count, group_blocks, rows, side), jnp.bfloat16),
            pltpu.VMEM((group_blocks + 1, rows, side), jnp.bfloat16),
            pltpu.VMEM(tiled, jnp.float32),
            pltpu.VMEM(tiled, jnp.float32),
            pltpu.VMEM((group_blocks, rows, side), jnp.bfloat16),
            dma((9,)),
            dma,
            dma((dp_count - 1,)),
            dma((dp_count - 1,)),
            dma((dp_count - 1,)),
            dma((dp_count - 1,)),
            pltpu.SemaphoreType.REGULAR,
            dma((2,)),
            dma((2,)),
            by_slot,
            by_slot,
            by_slot,
            by_slot,
        ],
        compiler_params=pltpu.CompilerParams(
            collective_id=0, has_side_effects=True, vmem_limit_bytes=LIMIT * 1024 * 1024
        ),
    )(
        owner_slot,
        grad_parts,
        moment,
        second,
        gram_left,
        gram_right,
        basis_left,
        basis_right,
    )
    return pl.pallas_call(
        hand_out_kernel,
        out_shape=out_shape,
        in_specs=[any_spec] * 5,
        out_specs=[any_spec] * 5,
        scratch_shapes=[dma((5,))],
        compiler_params=pltpu.CompilerParams(vmem_limit_bytes=8 * 1024 * 1024),
    )(*results)


def solution(mesh):
    by_slot = P(("dp", "fsdp"), None, None)
    return jax.shard_map(
        functools.partial(on_device, mesh.shape["dp"], mesh.shape["fsdp"]),
        mesh=mesh,
        in_specs=(P("dp", None, "fsdp", None), P()) + (by_slot,) * 6,
        out_specs=(by_slot,) * 4 + (P(None, "fsdp", None),),
        check_vma=False,
    )
```

```python
import functools
import math

import jax
import jax.numpy as jnp
from jax import lax
from jax.experimental import pallas as pl
from jax.experimental.pallas import tpu as pltpu
from jax.sharding import PartitionSpec as P

MESH = pl.DeviceIdType.MESH
UNROLL = 8
TILE = 8
LANES = 128
LIMIT = 60
PLANES = (1, 1, 1, 1, 4)


def contract(a, b, a_dim, b_dim):
    return lax.dot_general(
        a, b, (((a_dim,), (b_dim,)), ((), ())), preferred_element_type=jnp.float32
    )


def farthest_first(count, i):
    out = lax.div(i + 1, 2)
    return lax.rem(count // 2 + out * (1 - 2 * lax.rem(i, 2)) + count, count)


class Exchange:
    def __init__(self, dp, me, far, near, outgoing, incoming, sems):
        self.dp, self.me, self.far, self.near = dp, me, far, near
        self.outgoing, self.incoming, self.sems = outgoing, incoming, sems
        self.span = outgoing.shape[0] // (far * near)

    def copy(self, src, dst, target):
        return pltpu.make_async_remote_copy(
            src_ref=src,
            dst_ref=dst,
            send_sem=self.sems.at[0],
            recv_sem=self.sems.at[1],
            device_id=(self.dp, target),
            device_id_type=MESH,
        )

    def send(self, z, a):
        target = z * self.near + a
        self.copy(
            self.outgoing.at[pl.ds(target * self.span, self.span)],
            self.incoming.at[pl.ds(self.me * self.span, self.span)],
            target,
        ).start()

    def start(self, fill):
        chips = self.near // 2
        my_z, my_a = lax.div(self.me, self.near), lax.rem(self.me, self.near)
        my_y, my_core = lax.div(my_a, 2), lax.rem(my_a, 2)
        for total in range(self.far + chips - 1):

            def step(i, carry):
                z = lax.rem(my_z + farthest_first(self.far, i), self.far)
                y = lax.rem(my_y + farthest_first(chips, total - i), chips)
                for core in (1 - my_core, my_core):
                    fill(z, 2 * y + core)
                    self.send(z, 2 * y + core)
                return carry

            low, high = max(0, total - chips + 1), min(self.far - 1, total)
            if total < self.far + chips - 2:
                lax.fori_loop(low, high + 1, step, 0)
        fill(my_z, 2 * my_y + 1 - my_core)
        self.send(my_z, 2 * my_y + 1 - my_core)
        fill(my_z, my_a)
        for c in range(self.span):
            self.incoming[self.me * self.span + c] = self.outgoing[self.me * self.span + c]

    def start_by_z(self):
        chips = self.near // 2
        my_z, my_a = lax.div(self.me, self.near), lax.rem(self.me, self.near)
        my_y, my_core = lax.div(my_a, 2), lax.rem(my_a, 2)
        first = 0
        for planes in PLANES if sum(PLANES) == self.far else (1,) * self.far:

            def step(i, carry):
                z = first + lax.rem(my_z + i, planes)
                y = lax.rem(my_y + farthest_first(chips, lax.div(i, planes)), chips)
                self.send(z, 2 * y + 1 - my_core)

                @pl.when(jnp.logical_or(z != my_z, y != my_y))
                def _():
                    self.send(z, 2 * y + my_core)

                return carry

            lax.fori_loop(0, planes * chips, step, 0)
            first += planes
        for c in range(self.span):
            self.incoming[self.me * self.span + c] = self.outgoing[self.me * self.span + c]

    def whole(self):
        others = self.incoming.at[pl.ds(0, (self.far * self.near - 1) * self.span)]
        return self.copy(others, others, lax.rem(self.me + 1, self.far * self.near))


def soap_kernel(
    dp_count,
    far,
    near,
    owner_slot,
    grad_parts,
    moment,
    second,
    gram_left,
    gram_right,
    basis_left,
    basis_right,
    new_moment,
    new_second,
    new_left,
    new_right,
    update,
    owner_s,
    block_v,
    block_s,
    moment_v,
    second_v,
    left_v,
    right_v,
    basis_left_v,
    basis_right_v,
    partials,
    summed,
    slot_grad,
    slot_update,
    picked,
    load_sems,
    keep_sem,
    partial_send,
    partial_recv,
    gather_send,
    gather_recv,
    ready,
    out_sems,
    back_sems,
    outgoing,
    incoming,
    returning,
    returned,
):
    dp = lax.axis_index("dp")
    me = lax.axis_index("fsdp")
    capacity, side = moment.shape[0], moment.shape[1]
    group_blocks = owner_slot.shape[1]
    rows = grad_parts.shape[2]
    my_z, my_a = lax.div(me, near), lax.rem(me, near)
    outward = Exchange(dp, me, far, near, outgoing, incoming, out_sems)
    backward = Exchange(dp, me, far, near, returning, returned, back_sems)

    barrier = pltpu.get_barrier_semaphore()

    def greet(d, f):
        pl.semaphore_signal(barrier, inc=1, device_id=(d, f), device_id_type=MESH)

    for k in range(1, dp_count):
        greet(lax.rem(dp + k, dp_count), me)
    for k in range(1, near):
        greet(dp, my_z * near + lax.rem(my_a + k, near))
    for k in range(1, far):
        greet(dp, lax.rem(my_z + k, far) * near + my_a)

    own_partial = pltpu.make_async_copy(
        grad_parts.at[0, pl.ds(dp * group_blocks, group_blocks)], partials.at[0], load_sems.at[6]
    )
    own_partial.start()
    own_owners = pltpu.make_async_copy(owner_slot, owner_s, load_sems.at[7])
    own_owners.start()
    loads = [
        pltpu.make_async_copy(src, dst, load_sems.at[i])
        for i, (src, dst) in enumerate(
            (
                (basis_left, basis_left_v),
                (basis_right, basis_right_v),
                (moment, moment_v),
                (second, second_v),
                (gram_left, left_v),
                (gram_right, right_v),
            )
        )
    ]
    for load in loads:
        load.start()
    pl.semaphore_wait(barrier, dp_count - 1 + near - 1 + far - 1)

    dp_offsets = sorted(range(1, dp_count), key=lambda k: -min(k, dp_count - k))
    partial_copies = []
    for k in dp_offsets:
        target = lax.rem(dp + k, dp_count)
        copy = pltpu.make_async_remote_copy(
            src_ref=grad_parts.at[0, pl.ds(target * group_blocks, group_blocks)],
            dst_ref=partials.at[k],
            send_sem=partial_send.at[k - 1],
            recv_sem=partial_recv.at[k - 1],
            device_id=(target, me),
            device_id_type=MESH,
        )
        copy.start()
        partial_copies.append(copy)

    for k in range(1, near):
        pl.semaphore_signal(
            ready,
            inc=1,
            device_id=(dp, my_z * near + lax.rem(my_a + k, near)),
            device_id_type=MESH,
        )

    own_owners.wait()
    summed[group_blocks] = jnp.zeros(summed.shape[1:], summed.dtype)
    row_slots = near * capacity
    lane = lax.broadcasted_iota(jnp.int32, block_v.shape, 1)
    slot_id = row_slots * lax.broadcasted_iota(jnp.int32, block_v.shape, 0) + lane
    slot_id = jnp.where(lane < row_slots, slot_id, -1)

    def note(i, table):
        for u in range(UNROLL):
            j = i * UNROLL + u
            table = jnp.where(slot_id == owner_s[dp, j], j, table)
        return table

    block_v[...] = lax.fori_loop(
        0, group_blocks // UNROLL, note, jnp.full(block_v.shape, group_blocks, jnp.int32)
    )
    table_copy = pltpu.make_async_copy(block_v, block_s, load_sems.at[8])
    table_copy.start()

    own_partial.wait()
    for copy in partial_copies:
        copy.wait_recv()

    def add_up(i, carry):
        here = pl.ds(i * UNROLL, UNROLL)
        total = partials[0, here].astype(jnp.float32)
        for k in range(1, dp_count):
            total = total + partials[k, here].astype(jnp.float32)
        summed[here] = total.astype(jnp.bfloat16)
        return carry

    lax.fori_loop(0, group_blocks // UNROLL, add_up, 0)
    table_copy.wait()

    pl.semaphore_wait(ready, near - 1)

    def fill_grad(z, a):
        for c in range(capacity):
            outgoing[(z * near + a) * capacity + c] = summed[block_s[z, a * capacity + c]]

    outward.start(fill_grad)

    per_tile = TILE // rows
    tiles_near = near // per_tile

    def unpack(z, carry):
        for a in range(near):
            u = a % per_tile
            for c in range(capacity):
                slot_grad[c, z * tiles_near + a // per_tile, u * rows : (u + 1) * rows, :] = incoming[
                    (z * near + a) * capacity + c
                ].astype(jnp.float32)
        return carry

    for load in loads:
        load.wait()
    outward.whole().wait_recv()
    lax.fori_loop(0, far, unpack, 0)

    rounded = []
    for c in range(capacity):
        rounded.append(slot_grad[c].reshape(side, side).astype(jnp.bfloat16))
        halfway = contract(basis_left_v[c], rounded[c], 0, 0).astype(jnp.bfloat16)
        rotated = contract(halfway, basis_right_v[c], 1, 0)
        first_moment = 0.95 * moment_v[c].astype(jnp.float32) + 0.05 * rotated
        new_moment[c] = first_moment.astype(jnp.bfloat16)
        second_moment = 0.95 * second_v[c] + 0.05 * rotated * rotated
        new_second[c] = second_moment
        direct = (first_moment / (jnp.sqrt(second_moment) + 1e-8)).astype(jnp.bfloat16)
        back = contract(basis_left_v[c], direct, 1, 0).astype(jnp.bfloat16)
        slot_update[c] = contract(back, basis_right_v[c], 1, 1).reshape(slot_update.shape[1:])

    def pack(z, carry):
        for a in range(near):
            u = a % per_tile
            for c in range(capacity):
                returning[(z * near + a) * capacity + c] = slot_update[
                    c, z * tiles_near + a // per_tile, u * rows : (u + 1) * rows, :
                ].astype(jnp.bfloat16)
        return carry

    lax.fori_loop(0, far, pack, 0)
    backward.start_by_z()

    for c in range(capacity):
        new_left[c] = 0.95 * left_v[c] + 0.05 * contract(rounded[c], rounded[c], 1, 1)
        new_right[c] = 0.95 * right_v[c] + 0.05 * contract(rounded[c], rounded[c], 0, 0)
    backward.whole().wait_recv()

    def pick(i, carry):
        for u in range(UNROLL):
            picked[i * UNROLL + u] = returned[owner_s[dp, i * UNROLL + u]]
        return carry

    lax.fori_loop(0, group_blocks // UNROLL, pick, 0)

    mine = pl.ds(dp * group_blocks, group_blocks)
    gathers = []
    for k in dp_offsets:
        copy = pltpu.make_async_remote_copy(
            src_ref=picked,
            dst_ref=update.at[mine],
            send_sem=gather_send.at[k - 1],
            recv_sem=gather_recv.at[k - 1],
            device_id=(lax.rem(dp + k, dp_count), me),
            device_id_type=MESH,
        )
        copy.start()
        gathers.append(copy)
    keep = pltpu.make_async_copy(picked, update.at[mine], keep_sem)
    keep.start()
    outward.whole().wait_send()
    backward.whole().wait_send()
    for copy in partial_copies:
        copy.wait_send()
    keep.wait()
    for copy in gathers:
        copy.wait()


def hand_out_kernel(*refs):
    count = len(refs) // 2
    sems = refs[-1]
    copies = [
        pltpu.make_async_copy(src, dst, sems.at[i])
        for i, (src, dst) in enumerate(zip(refs[:count], refs[count : 2 * count]))
    ]
    for copy in copies:
        copy.start()
    for copy in copies:
        copy.wait()


def on_device(
    dp_count,
    fsdp_count,
    grad_parts,
    owner_slot,
    moment,
    second,
    gram_left,
    gram_right,
    basis_left,
    basis_right,
):
    capacity, side = moment.shape[0], moment.shape[1]
    blocks, rows = grad_parts.shape[1], grad_parts.shape[2]
    group_blocks = owner_slot.shape[1]
    far = math.isqrt(fsdp_count // 2)
    near = fsdp_count // far
    any_spec = pl.BlockSpec(memory_space=pl.ANY)
    square = (capacity, side, side)
    tiled = (capacity, side // TILE, TILE, side)
    by_slot = pltpu.VMEM((fsdp_count * capacity, rows, side), jnp.bfloat16)
    table = (-(-far // TILE) * TILE, LANES)
    dma = pltpu.SemaphoreType.DMA
    out_shape = (
        jax.ShapeDtypeStruct(square, jnp.bfloat16),
        jax.ShapeDtypeStruct(square, jnp.float32),
        jax.ShapeDtypeStruct(square, jnp.float32),
        jax.ShapeDtypeStruct(square, jnp.float32),
        jax.ShapeDtypeStruct((blocks, rows, side), jnp.bfloat16),
    )
    results = pl.pallas_call(
        functools.partial(soap_kernel, dp_count, far, near),
        out_shape=tuple(pltpu.VMEM(out.shape, out.dtype) for out in out_shape),
        in_specs=[any_spec] * 8,
        out_specs=[pl.BlockSpec(memory_space=pltpu.VMEM)] * 5,
        scratch_shapes=[
            pltpu.SMEM(owner_slot.shape, jnp.int32),
            pltpu.VMEM(table, jnp.int32),
            pltpu.SMEM(table, jnp.int32),
            pltpu.VMEM(square, jnp.bfloat16),
            pltpu.VMEM(square, jnp.float32),
            pltpu.VMEM(square, jnp.float32),
            pltpu.VMEM(square, jnp.float32),
            pltpu.VMEM(square, jnp.bfloat16),
            pltpu.VMEM(square, jnp.bfloat16),
            pltpu.VMEM((dp_count, group_blocks, rows, side), jnp.bfloat16),
            pltpu.VMEM((group_blocks + 1, rows, side), jnp.bfloat16),
            pltpu.VMEM(tiled, jnp.float32),
            pltpu.VMEM(tiled, jnp.float32),
            pltpu.VMEM((group_blocks, rows, side), jnp.bfloat16),
            dma((9,)),
            dma,
            dma((dp_count - 1,)),
            dma((dp_count - 1,)),
            dma((dp_count - 1,)),
            dma((dp_count - 1,)),
            pltpu.SemaphoreType.REGULAR,
            dma((2,)),
            dma((2,)),
            by_slot,
            by_slot,
            by_slot,
            by_slot,
        ],
        compiler_params=pltpu.CompilerParams(
            collective_id=0, has_side_effects=True, vmem_limit_bytes=LIMIT * 1024 * 1024
        ),
    )(
        owner_slot,
        grad_parts,
        moment,
        second,
        gram_left,
        gram_right,
        basis_left,
        basis_right,
    )
    return pl.pallas_call(
        hand_out_kernel,
        out_shape=out_shape,
        in_specs=[any_spec] * 5,
        out_specs=[any_spec] * 5,
        scratch_shapes=[dma((5,))],
        compiler_params=pltpu.CompilerParams(vmem_limit_bytes=8 * 1024 * 1024),
    )(*results)


def solution(mesh):
    by_slot = P(("dp", "fsdp"), None, None)
    return jax.shard_map(
        functools.partial(on_device, mesh.shape["dp"], mesh.shape["fsdp"]),
        mesh=mesh,
        in_specs=(P("dp", None, "fsdp", None), P()) + (by_slot,) * 6,
        out_specs=(by_slot,) * 4 + (P(None, "fsdp", None),),
        check_vma=False,
    )
```

```python
import functools
import math

import jax
import jax.numpy as jnp
from jax import lax
from jax.experimental import pallas as pl
from jax.experimental.pallas import tpu as pltpu
from jax.sharding import PartitionSpec as P

MESH = pl.DeviceIdType.MESH
UNROLL = 8
TILE = 8
LANES = 128
LIMIT = 60
PLANES = (1, 1, 1, 1, 4)


def contract(a, b, a_dim, b_dim):
    return lax.dot_general(
        a, b, (((a_dim,), (b_dim,)), ((), ())), preferred_element_type=jnp.float32
    )


def farthest_first(count, i):
    out = lax.div(i + 1, 2)
    return lax.rem(count // 2 + out * (1 - 2 * lax.rem(i, 2)) + count, count)


class Exchange:
    def __init__(self, dp, me, far, near, outgoing, incoming, sems):
        self.dp, self.me, self.far, self.near = dp, me, far, near
        self.outgoing, self.incoming, self.sems = outgoing, incoming, sems
        self.span = outgoing.shape[0] // (far * near)

    def copy(self, src, dst, target):
        return pltpu.make_async_remote_copy(
            src_ref=src,
            dst_ref=dst,
            send_sem=self.sems.at[0],
            recv_sem=self.sems.at[1],
            device_id=(self.dp, target),
            device_id_type=MESH,
        )

    def send(self, z, a):
        target = z * self.near + a
        self.copy(
            self.outgoing.at[pl.ds(target * self.span, self.span)],
            self.incoming.at[pl.ds(self.me * self.span, self.span)],
            target,
        ).start()

    def start(self, fill):
        chips = self.near // 2
        my_z, my_a = lax.div(self.me, self.near), lax.rem(self.me, self.near)
        my_y, my_core = lax.div(my_a, 2), lax.rem(my_a, 2)
        for total in range(self.far + chips - 1):

            def step(i, carry):
                z = lax.rem(my_z + farthest_first(self.far, i), self.far)
                y = lax.rem(my_y + farthest_first(chips, total - i), chips)
                for core in (1 - my_core, my_core):
                    fill(z, 2 * y + core)
                    self.send(z, 2 * y + core)
                return carry

            low, high = max(0, total - chips + 1), min(self.far - 1, total)
            if total < self.far + chips - 2:
                lax.fori_loop(low, high + 1, step, 0)
        fill(my_z, 2 * my_y + 1 - my_core)
        self.send(my_z, 2 * my_y + 1 - my_core)
        fill(my_z, my_a)
        for c in range(self.span):
            self.incoming[self.me * self.span + c] = self.outgoing[self.me * self.span + c]

    def start_by_z(self):
        chips = self.near // 2
        my_z, my_a = lax.div(self.me, self.near), lax.rem(self.me, self.near)
        my_y, my_core = lax.div(my_a, 2), lax.rem(my_a, 2)
        first = 0
        for planes in PLANES if sum(PLANES) == self.far else (1,) * self.far:

            def step(i, carry):
                z = first + lax.rem(my_z + i, planes)
                y = lax.rem(my_y + farthest_first(chips, lax.div(i, planes)), chips)
                self.send(z, 2 * y + 1 - my_core)

                @pl.when(jnp.logical_or(z != my_z, y != my_y))
                def _():
                    self.send(z, 2 * y + my_core)

                return carry

            lax.fori_loop(0, planes * chips, step, 0)
            first += planes
        for c in range(self.span):
            self.incoming[self.me * self.span + c] = self.outgoing[self.me * self.span + c]

    def whole(self):
        others = self.incoming.at[pl.ds(0, (self.far * self.near - 1) * self.span)]
        return self.copy(others, others, lax.rem(self.me + 1, self.far * self.near))


def soap_kernel(
    dp_count,
    far,
    near,
    owner_slot,
    grad_parts,
    moment,
    second,
    gram_left,
    gram_right,
    basis_left,
    basis_right,
    new_moment,
    new_second,
    new_left,
    new_right,
    update,
    owner_s,
    block_v,
    block_s,
    moment_v,
    second_v,
    left_v,
    right_v,
    basis_left_v,
    basis_right_v,
    partials,
    summed,
    slot_grad,
    slot_update,
    picked,
    load_sems,
    keep_sem,
    partial_send,
    partial_recv,
    gather_send,
    gather_recv,
    ready,
    out_sems,
    back_sems,
    outgoing,
    incoming,
    returning,
    returned,
):
    dp = lax.axis_index("dp")
    me = lax.axis_index("fsdp")
    capacity, side = moment.shape[0], moment.shape[1]
    group_blocks = owner_slot.shape[1]
    rows = grad_parts.shape[2]
    my_z, my_a = lax.div(me, near), lax.rem(me, near)
    outward = Exchange(dp, me, far, near, outgoing, incoming, out_sems)
    backward = Exchange(dp, me, far, near, returning, returned, back_sems)

    barrier = pltpu.get_barrier_semaphore()

    def greet(d, f):
        pl.semaphore_signal(barrier, inc=1, device_id=(d, f), device_id_type=MESH)

    for k in range(1, dp_count):
        greet(lax.rem(dp + k, dp_count), me)
    for k in range(1, near):
        greet(dp, my_z * near + lax.rem(my_a + k, near))
    for k in range(1, far):
        greet(dp, lax.rem(my_z + k, far) * near + my_a)

    own_partial = pltpu.make_async_copy(
        grad_parts.at[0, pl.ds(dp * group_blocks, group_blocks)], partials.at[0], load_sems.at[6]
    )
    own_partial.start()
    own_owners = pltpu.make_async_copy(owner_slot, owner_s, load_sems.at[7])
    own_owners.start()
    loads = [
        pltpu.make_async_copy(src, dst, load_sems.at[i])
        for i, (src, dst) in enumerate(
            (
                (basis_left, basis_left_v),
                (basis_right, basis_right_v),
                (moment, moment_v),
                (second, second_v),
                (gram_left, left_v),
                (gram_right, right_v),
            )
        )
    ]
    for load in loads:
        load.start()
    pl.semaphore_wait(barrier, dp_count - 1 + near - 1 + far - 1)

    dp_offsets = sorted(range(1, dp_count), key=lambda k: -min(k, dp_count - k))
    partial_copies = []
    for k in dp_offsets:
        target = lax.rem(dp + k, dp_count)
        copy = pltpu.make_async_remote_copy(
            src_ref=grad_parts.at[0, pl.ds(target * group_blocks, group_blocks)],
            dst_ref=partials.at[k],
            send_sem=partial_send.at[k - 1],
            recv_sem=partial_recv.at[k - 1],
            device_id=(target, me),
            device_id_type=MESH,
        )
        copy.start()
        partial_copies.append(copy)

    for k in range(1, near):
        pl.semaphore_signal(
            ready,
            inc=1,
            device_id=(dp, my_z * near + lax.rem(my_a + k, near)),
            device_id_type=MESH,
        )

    own_owners.wait()
    summed[group_blocks] = jnp.zeros(summed.shape[1:], summed.dtype)
    row_slots = near * capacity
    lane = lax.broadcasted_iota(jnp.int32, block_v.shape, 1)
    slot_id = row_slots * lax.broadcasted_iota(jnp.int32, block_v.shape, 0) + lane
    slot_id = jnp.where(lane < row_slots, slot_id, -1)

    def note(i, table):
        for u in range(UNROLL):
            j = i * UNROLL + u
            table = jnp.where(slot_id == owner_s[dp, j], j, table)
        return table

    block_v[...] = lax.fori_loop(
        0, group_blocks // UNROLL, note, jnp.full(block_v.shape, group_blocks, jnp.int32)
    )
    table_copy = pltpu.make_async_copy(block_v, block_s, load_sems.at[8])
    table_copy.start()

    own_partial.wait()
    for copy in partial_copies:
        copy.wait_recv()

    def add_up(i, carry):
        here = pl.ds(i * UNROLL, UNROLL)
        total = partials[0, here].astype(jnp.float32)
        for k in range(1, dp_count):
            total = total + partials[k, here].astype(jnp.float32)
        summed[here] = total.astype(jnp.bfloat16)
        return carry

    lax.fori_loop(0, group_blocks // UNROLL, add_up, 0)
    table_copy.wait()

    pl.semaphore_wait(ready, near - 1)

    def fill_grad(z, a):
        for c in range(capacity):
            outgoing[(z * near + a) * capacity + c] = summed[block_s[z, a * capacity + c]]

    outward.start(fill_grad)

    per_tile = TILE // rows
    tiles_near = near // per_tile

    def unpack(z, carry):
        for a in range(near):
            u = a % per_tile
            for c in range(capacity):
                slot_grad[c, z * tiles_near + a // per_tile, u * rows : (u + 1) * rows, :] = incoming[
                    (z * near + a) * capacity + c
                ].astype(jnp.float32)
        return carry

    for load in loads:
        load.wait()
    outward.whole().wait_recv()
    lax.fori_loop(0, far, unpack, 0)

    every = range(capacity)
    rounded = [slot_grad[c].reshape(side, side).astype(jnp.bfloat16) for c in every]
    halfway = [contract(basis_left_v[c], rounded[c], 0, 0).astype(jnp.bfloat16) for c in every]
    rotated = [contract(halfway[c], basis_right_v[c], 1, 0) for c in every]
    direct = []
    for c in every:
        first_moment = 0.95 * moment_v[c].astype(jnp.float32) + 0.05 * rotated[c]
        second_moment = 0.95 * second_v[c] + 0.05 * rotated[c] * rotated[c]
        new_moment[c] = first_moment.astype(jnp.bfloat16)
        new_second[c] = second_moment
        direct.append((first_moment / (jnp.sqrt(second_moment) + 1e-8)).astype(jnp.bfloat16))
    back = [contract(basis_left_v[c], direct[c], 1, 0).astype(jnp.bfloat16) for c in every]
    for c in every:
        slot_update[c] = contract(back[c], basis_right_v[c], 1, 1).reshape(slot_update.shape[1:])

    def pack(z, carry):
        for a in range(near):
            u = a % per_tile
            for c in range(capacity):
                returning[(z * near + a) * capacity + c] = slot_update[
                    c, z * tiles_near + a // per_tile, u * rows : (u + 1) * rows, :
                ].astype(jnp.bfloat16)
        return carry

    lax.fori_loop(0, far, pack, 0)
    backward.start_by_z()

    for c in range(capacity):
        new_left[c] = 0.95 * left_v[c] + 0.05 * contract(rounded[c], rounded[c], 1, 1)
        new_right[c] = 0.95 * right_v[c] + 0.05 * contract(rounded[c], rounded[c], 0, 0)
    backward.whole().wait_recv()

    def pick(i, carry):
        for u in range(UNROLL):
            picked[i * UNROLL + u] = returned[owner_s[dp, i * UNROLL + u]]
        return carry

    lax.fori_loop(0, group_blocks // UNROLL, pick, 0)

    mine = pl.ds(dp * group_blocks, group_blocks)
    gathers = []
    for k in dp_offsets:
        copy = pltpu.make_async_remote_copy(
            src_ref=picked,
            dst_ref=update.at[mine],
            send_sem=gather_send.at[k - 1],
            recv_sem=gather_recv.at[k - 1],
            device_id=(lax.rem(dp + k, dp_count), me),
            device_id_type=MESH,
        )
        copy.start()
        gathers.append(copy)
    keep = pltpu.make_async_copy(picked, update.at[mine], keep_sem)
    keep.start()
    outward.whole().wait_send()
    backward.whole().wait_send()
    for copy in partial_copies:
        copy.wait_send()
    keep.wait()
    for copy in gathers:
        copy.wait()


def hand_out_kernel(*refs):
    count = len(refs) // 2
    sems = refs[-1]
    copies = [
        pltpu.make_async_copy(src, dst, sems.at[i])
        for i, (src, dst) in enumerate(zip(refs[:count], refs[count : 2 * count]))
    ]
    for copy in copies:
        copy.start()
    for copy in copies:
        copy.wait()


def on_device(
    dp_count,
    fsdp_count,
    grad_parts,
    owner_slot,
    moment,
    second,
    gram_left,
    gram_right,
    basis_left,
    basis_right,
):
    capacity, side = moment.shape[0], moment.shape[1]
    blocks, rows = grad_parts.shape[1], grad_parts.shape[2]
    group_blocks = owner_slot.shape[1]
    far = math.isqrt(fsdp_count // 2)
    near = fsdp_count // far
    any_spec = pl.BlockSpec(memory_space=pl.ANY)
    square = (capacity, side, side)
    tiled = (capacity, side // TILE, TILE, side)
    by_slot = pltpu.VMEM((fsdp_count * capacity, rows, side), jnp.bfloat16)
    table = (-(-far // TILE) * TILE, LANES)
    dma = pltpu.SemaphoreType.DMA
    out_shape = (
        jax.ShapeDtypeStruct(square, jnp.bfloat16),
        jax.ShapeDtypeStruct(square, jnp.float32),
        jax.ShapeDtypeStruct(square, jnp.float32),
        jax.ShapeDtypeStruct(square, jnp.float32),
        jax.ShapeDtypeStruct((blocks, rows, side), jnp.bfloat16),
    )
    results = pl.pallas_call(
        functools.partial(soap_kernel, dp_count, far, near),
        out_shape=tuple(pltpu.VMEM(out.shape, out.dtype) for out in out_shape),
        in_specs=[any_spec] * 8,
        out_specs=[pl.BlockSpec(memory_space=pltpu.VMEM)] * 5,
        scratch_shapes=[
            pltpu.SMEM(owner_slot.shape, jnp.int32),
            pltpu.VMEM(table, jnp.int32),
            pltpu.SMEM(table, jnp.int32),
            pltpu.VMEM(square, jnp.bfloat16),
            pltpu.VMEM(square, jnp.float32),
            pltpu.VMEM(square, jnp.float32),
            pltpu.VMEM(square, jnp.float32),
            pltpu.VMEM(square, jnp.bfloat16),
            pltpu.VMEM(square, jnp.bfloat16),
            pltpu.VMEM((dp_count, group_blocks, rows, side), jnp.bfloat16),
            pltpu.VMEM((group_blocks + 1, rows, side), jnp.bfloat16),
            pltpu.VMEM(tiled, jnp.float32),
            pltpu.VMEM(tiled, jnp.float32),
            pltpu.VMEM((group_blocks, rows, side), jnp.bfloat16),
            dma((9,)),
            dma,
            dma((dp_count - 1,)),
            dma((dp_count - 1,)),
            dma((dp_count - 1,)),
            dma((dp_count - 1,)),
            pltpu.SemaphoreType.REGULAR,
            dma((2,)),
            dma((2,)),
            by_slot,
            by_slot,
            by_slot,
            by_slot,
        ],
        compiler_params=pltpu.CompilerParams(
            collective_id=0, has_side_effects=True, vmem_limit_bytes=LIMIT * 1024 * 1024
        ),
    )(
        owner_slot,
        grad_parts,
        moment,
        second,
        gram_left,
        gram_right,
        basis_left,
        basis_right,
    )
    return pl.pallas_call(
        hand_out_kernel,
        out_shape=out_shape,
        in_specs=[any_spec] * 5,
        out_specs=[any_spec] * 5,
        scratch_shapes=[dma((5,))],
        compiler_params=pltpu.CompilerParams(vmem_limit_bytes=8 * 1024 * 1024),
    )(*results)


def solution(mesh):
    by_slot = P(("dp", "fsdp"), None, None)
    return jax.shard_map(
        functools.partial(on_device, mesh.shape["dp"], mesh.shape["fsdp"]),
        mesh=mesh,
        in_specs=(P("dp", None, "fsdp", None), P()) + (by_slot,) * 6,
        out_specs=(by_slot,) * 4 + (P(None, "fsdp", None),),
        check_vma=False,
    )
```
